256 devices in a mesh: chord: 16 (over z_hi, x), span: 16 (over y, z_lo, core).
Axes of the slice: x: 4, y: 4, z: 8 (z_hi: 4, z_lo: 2; z = z_hi * 2 + z_lo), core: 2. Of those that a mesh axis runs over, the one named last changes fastest.
Arguments:
- adjoint: float32 [6, 32, 128, 256], P(None, 'chord', 'span'), may hold values from -6 to 6
- source: float32 [6, 32, 128, 256], P(None, 'chord', 'span'), may hold values from -24 to 24
- diag_block: bfloat16 [6, 6, 32, 128, 256], P(None, None, 'chord', 'span'), as said below
- couplings: bfloat16 [6, 6, 6, 32, 128, 256], P(None, None, None, 'chord', 'span'), may hold values from -1.1953125 to 1.1953125
- line_inverse: bfloat16 [6, 6, 2, 32, 128, 256], P(None, None, None, 'chord', 'span')
- partner: int32 [32], P('chord'), may hold values from -1 to 31, as said below
- codes: int32 [32, 128], P('chord', 'span'), may hold values from 0 to 1
Outputs:
- adjoint_out: float32 [6, 32, 128, 256], P(None, 'chord', 'span')
- residual: float32 [6, 32, 128, 256], P(None, 'chord', 'span')
The draws below stay inside these ranges and needn't reach their ends.
Inputs may be any that keep to these rules, and one draw needn't show every extreme that they name: partner[i] is either -1 or 31 - i; partner[i] >= 0 exactly when partner[31 - i] >= 0; partner[0] >= 0. The diagonal entries of diag_block lie in 3 to 9.
All inputs are finite; a program needn't handle non-finite values.
Results may differ from the reference program's by a relative error of at most 0.0006.
Values may be sent and summed in bfloat16 or wider, within the bound.
No kernel may reach another device: no remote copies, remote signals or barrier semaphores. Data moves between devices by JAX's collectives and lax.ppermute only.
A program may use at most 64 MiB of HBM per device.

```python
import jax
import jax.numpy as jnp
from jax import lax

N = 256
SWEEPS = 6
NC = 32
NS = 128


def diagonal_values(key):
    return jnp.exp(jax.random.uniform(key, (6, NC, NS, N), jnp.float32, jnp.log(3.0), jnp.log(9.0)))


def draw_diag_block(key, part):
    values = diagonal_values(key)
    key = jax.random.fold_in(key, 11)
    identity = jnp.eye(6, dtype=jnp.float32)[:, :, None, None, None]
    others = 0.6 * jax.random.normal(key, (6, 6, NC, NS, N), jnp.float32)
    blocks = identity * values[:, None] + (1.0 - identity) * others
    return blocks.astype(jnp.bfloat16)


def draw_line_inverse(key, part):
    values = diagonal_values(key)
    key = jax.random.fold_in(key, 12)
    identity = jnp.eye(6, dtype=jnp.float32)[:, :, None, None, None, None]
    offset = jnp.arange(2)[:, None, None, None] == (jnp.arange(N) % 2)[None, None, None, :]
    own_point = identity * offset.astype(jnp.float32)[None, None]
    others = 0.03 * jax.random.normal(key, (6, 6, 2, NC, NS, N), jnp.float32)
    blocks = own_point * (0.8 / values)[:, None, None] + (1.0 - own_point) * others
    return blocks.astype(jnp.bfloat16)


def draw_partner(key, part):
    key = jax.random.fold_in(key, 13)
    reach = jax.random.randint(key, (), NC // 8, 3 * NC // 8 + 1)
    position = jnp.arange(NC, dtype=jnp.int32)
    in_wake = (position < reach) | (position >= NC - reach)
    return jnp.where(in_wake, NC - 1 - position, -1).astype(jnp.int32)


def set_ends(entries, own_key, least, largest):
    extent = entries.shape
    spot = [jax.random.randint(jax.random.fold_in(own_key, axis), (), 0, extent[axis]) for axis in range(len(extent))]
    entries = entries.at[tuple(spot)].set(least)
    longest = extent.index(max(extent))
    spot[longest] = (spot[longest] + 1) % extent[longest]
    return entries.at[tuple(spot)].set(largest)


def levels(stream_key, dims, cuts, least, largest):
    def one(axis_at, shards_of):
        heights = jax.random.uniform(jax.random.fold_in(jax.random.fold_in(stream_key, 6), axis_at), (shards_of,), jnp.float32, least / len(cuts), largest / len(cuts))
        return jnp.repeat(jnp.exp(heights), dims[axis_at] // shards_of).reshape((-1,) + (1,) * (len(dims) - axis_at - 1))

    factor_of = one(*cuts[0])
    for cut in cuts[1:]:
        factor_of = factor_of * one(*cut)
    return factor_of


def normal_values(stream_key, dims, scale, most, pieces=(), held_as=jnp.bfloat16):
    entries = scale * jax.random.normal(stream_key, dims, jnp.float32)
    if pieces:
        entries = entries * levels(stream_key, dims, pieces, -0.22, 0.18)
    return jnp.clip(entries, -most, most).astype(held_as)


def setup_inputs(seed: int = 0) -> dict:
    key_list = jax.random.split(jax.random.key(seed), 8)
    adjoint = normal_values(key_list[0], (6, NC, NS, N), 1.0, 6.0, ((1, 16), (2, 16)), jnp.float32)
    source = normal_values(key_list[1], (6, NC, NS, N), 4.0, 24.0, ((1, 16), (2, 16)), jnp.float32)
    diag_block = draw_diag_block(jax.random.fold_in(key_list[7], 71), 0)
    couplings = normal_values(key_list[3], (6, 6, 6, NC, NS, N), 0.2, 1.1953125, ((3, 16), (4, 16)))
    line_inverse = draw_line_inverse(jax.random.fold_in(key_list[7], 71), 0)
    partner = draw_partner(jax.random.fold_in(key_list[7], 71), 0)
    codes = set_ends(jax.random.randint(key_list[6], (NC, NS), 0, 2), jax.random.fold_in(key_list[6], 1), 0, 1).astype(jnp.int32)
    return dict(adjoint=adjoint, source=source, diag_block=diag_block, couplings=couplings, line_inverse=line_inverse, partner=partner, codes=codes)


def block_product(blocks, field):
    return jnp.einsum("abcsn,acsn->bcsn", blocks.astype(jnp.float32), field, precision=lax.Precision.HIGHEST)


def shift_down(values, dimension):
    padding = [(0, 0)] * values.ndim
    padding[dimension] = (1, 0)
    return jnp.pad(lax.slice_in_dim(values, 0, values.shape[dimension] - 1, axis=dimension), padding)


def shift_up(values, dimension):
    padding = [(0, 0)] * values.ndim
    padding[dimension] = (0, 1)
    return jnp.pad(lax.slice_in_dim(values, 1, values.shape[dimension], axis=dimension), padding)


def wall_keep(partner, codes):
    wall_cell = (partner < 0)[:, None]
    component = jnp.arange(6)[:, None, None]
    velocity = (component >= 1) & (component <= 3)
    dropped = wall_cell[None] & ((component == 5) | (velocity & (codes[None] == 0)))
    return jnp.where(dropped, 0.0, 1.0).astype(jnp.float32)


def line_update(line_inverse, residual):
    count_state, count_chord, count_span, count_line = residual.shape
    pairs = residual.reshape(count_state, count_chord, count_span, count_line // 2, 2)
    spread = jnp.broadcast_to(jnp.moveaxis(pairs, 4, 1)[..., None], (count_state, 2, count_chord, count_span, count_line // 2, 2))
    spread = spread.reshape(count_state, 2, count_chord, count_span, count_line)
    return jnp.einsum("abqcsn,bqcsn->acsn", line_inverse.astype(jnp.float32), spread, precision=lax.Precision.HIGHEST)


def reference(adjoint, source, diag_block, couplings, line_inverse, partner, codes):
    keeping = wall_keep(partner, codes)
    has_partner = partner >= 0
    partner_index = jnp.where(has_partner, partner, 0).astype(jnp.int32)
    residual = source
    for repeat in range(SWEEPS):
        applied = block_product(diag_block, adjoint)
        applied = applied + shift_down(block_product(couplings[1], adjoint), 1)
        applied = applied + shift_up(block_product(couplings[0], adjoint), 1)
        applied = applied + shift_down(block_product(couplings[3], adjoint), 2)
        applied = applied + shift_up(block_product(couplings[2], adjoint), 2)
        normal_minus = block_product(couplings[4], adjoint)
        applied = applied + shift_down(block_product(couplings[5], adjoint), 3) + shift_up(normal_minus, 3)
        cut_row = normal_minus[:, :, :, 0]
        mirrored = cut_row[:, partner_index]
        applied = applied.at[:, :, :, 0].add(jnp.where(has_partner[None, :, None], mirrored, 0.0))
        residual = source - applied
        residual = residual.at[:, :, :, 0].multiply(keeping)
        adjoint = adjoint + line_update(line_inverse, residual)
    return adjoint, residual
```

```python
import jax
import jax.numpy as jnp
from jax import lax
from jax.experimental import pallas as pl
from jax.experimental.pallas import tpu as pltpu
from jax.sharding import PartitionSpec as P

SWEEPS = 6
F32 = jnp.float32
VMEM_LIMIT = 24 * 2**20


def product(blocks, lead, field):
    out = [None] * 6
    for a in range(6):
        for b in range(6):
            term = blocks[(*lead, a, b)].astype(F32) * field[a]
            out[b] = term if a == 0 else out[b] + term
    return out


def product_rows(blocks, lead, field, low):
    out = [None] * 6
    for a in range(6):
        for b in range(6):
            term = blocks[(*lead, a, b)].astype(F32)[low : low + 8] * field[a][low : low + 8]
            out[b] = term if a == 0 else out[b] + term
    return out


def iotas(shape):
    return lax.broadcasted_iota(jnp.int32, shape, 0), lax.broadcasted_iota(jnp.int32, shape, 1)


def edges(source, couplings, field, even_chord, even_span, out):
    part_ref, chord_even_ref, chord_odd_ref, span_even_ref, span_odd_ref, cut_ref = out
    up = product_rows(couplings, (1,), field, 8)
    down = product_rows(couplings, (0,), field, 0)
    for b in range(6):
        chord_odd_ref[b] = jnp.where(even_chord, down[b], up[b])
        chord_even_ref[b] = jnp.where(even_chord, up[b], down[b])
    plus = product(couplings, (3,), field)
    minus = product(couplings, (2,), field)
    for b in range(6):
        for c in range(2):
            top, bottom = (minus[b][8 * c : 8 * c + 1], plus[b][8 * c + 7 : 8 * c + 8])
            at = 2 * b + c
            span_odd_ref[at : at + 1] = jnp.where(even_span, top, bottom)
            span_even_ref[at : at + 1] = jnp.where(even_span, bottom, top)
    normal = product(couplings, (4,), field)
    row, lane = iotas((16, 256))
    row = row % 8
    cut = jnp.zeros((8, 128), F32)
    cut_lane = iotas((8, 128))[1]
    for b in range(6):
        for c in range(2):
            column = normal[b][8 * c : 8 * c + 8, 0:1]
            cut = jnp.where(cut_lane == 2 * b + c, column, cut)
    cut_ref[...] = cut
    for b in range(6):
        inside = jnp.where(row == 0, 0.0, pltpu.roll(plus[b], 1, 0))
        inside = inside + jnp.where(row == 7, 0.0, pltpu.roll(minus[b], 15, 0))
        inside = inside + jnp.where(lane == 255, 0.0, pltpu.roll(normal[b], 255, 1))
        part_ref[b] = source[b] - inside


def first_kernel(source, couplings, adjoint, *out):
    even_chord = lax.axis_index("chord") % 2 == 0
    even_span = lax.axis_index("span") % 2 == 0
    field = [adjoint[a] for a in range(6)]
    edges(source, couplings, field, even_chord, even_span, out)


def inside_kernel(part, diag_block, couplings, adjoint, out):
    field = [adjoint[a] for a in range(6)]
    own = product(diag_block, (), field)
    up = product_rows(couplings, (1,), field, 0)
    down = product_rows(couplings, (0,), field, 8)
    normal = product(couplings, (5,), field)
    lane = iotas((16, 256))[1]
    for b in range(6):
        inside = own[b] + jnp.where(lane == 0, 0.0, pltpu.roll(normal[b], 1, 1))
        inside = inside + jnp.concatenate([down[b], up[b]], axis=0)
        out[b] = part[b] - inside


def finish(part, got, masks, line_inverse, adjoint, even_chord, even_span):
    chord_even, chord_odd, span_even, span_odd, cut = got
    row, lane = iotas((16, 256))
    row = row % 8
    top = jnp.where(even_span, span_odd[...], span_even[...])
    bottom = jnp.where(even_span, span_even[...], span_odd[...])
    arrived = cut[...]
    odd_lane = lane % 2 == 1
    residual, even_part, odd_part = [], [], []
    for b in range(6):
        ev, od = chord_even[b], chord_odd[b]
        outside = jnp.concatenate([jnp.where(even_chord, od, ev), jnp.where(even_chord, ev, od)], axis=0)
        tops = jnp.concatenate(
            [jnp.broadcast_to(top[2 * b + c : 2 * b + c + 1], (8, 256)) for c in range(2)], axis=0
        )
        bottoms = jnp.concatenate(
            [jnp.broadcast_to(bottom[2 * b + c : 2 * b + c + 1], (8, 256)) for c in range(2)], axis=0
        )
        outside = outside + jnp.where(row == 0, tops, jnp.where(row == 7, bottoms, 0.0))
        columns = jnp.concatenate([arrived[:, 2 * b + 1 : 2 * b + 2], arrived[:, 2 * b : 2 * b + 1]], axis=0)
        outside = outside + jnp.where((lane == 0) & (masks[2][:, 0:1] > 0), columns, 0.0)
        value = part[b] - outside
        if 1 <= b <= 3:
            value = value * jnp.where(lane == 0, masks[0][:, 0:1], 1.0)
        if b == 5:
            value = value * jnp.where(lane == 0, masks[1][:, 0:1], 1.0)
        residual.append(value)
        even_part.append(jnp.where(odd_lane, pltpu.roll(value, 1, 1), value))
        odd_part.append(jnp.where(odd_lane, value, pltpu.roll(value, 255, 1)))
    after = []
    for a in range(6):
        total = adjoint[a]
        for b in range(6):
            total = total + line_inverse[a, b, 0].astype(F32) * even_part[b]
            total = total + line_inverse[a, b, 1].astype(F32) * odd_part[b]
        after.append(total)
    return residual, after


def middle_kernel(
    part, chord_even, chord_odd, span_even, span_odd, cut, masks, line_inverse, adjoint, source, couplings, after_ref, *out
):
    even_chord = lax.axis_index("chord") % 2 == 0
    even_span = lax.axis_index("span") % 2 == 0
    got = (chord_even, chord_odd, span_even, span_odd, cut)
    _, after = finish(part, got, masks, line_inverse, adjoint, even_chord, even_span)
    for a in range(6):
        after_ref[a] = after[a]
    edges(source, couplings, after, even_chord, even_span, out)


def last_kernel(
    part, chord_even, chord_odd, span_even, span_odd, cut, masks, line_inverse, adjoint, after_ref, residual_ref
):
    even_chord = lax.axis_index("chord") % 2 == 0
    even_span = lax.axis_index("span") % 2 == 0
    got = (chord_even, chord_odd, span_even, span_odd, cut)
    residual, after = finish(part, got, masks, line_inverse, adjoint, even_chord, even_span)
    for a in range(6):
        after_ref[a] = after[a]
        residual_ref[a] = residual[a]


def call(kernel, name, operands, shapes, flops, in_vmem=True):
    vmem = pl.BlockSpec(memory_space=pltpu.VMEM)
    made = [pltpu.VMEM(s, F32) if in_vmem else jax.ShapeDtypeStruct(s, F32) for s in shapes]
    held = [pltpu.with_memory_space_constraint(x, pltpu.VMEM) for x in operands]
    return pl.pallas_call(
        kernel,
        name=name,
        out_shape=made,
        in_specs=[vmem] * len(held),
        out_specs=[vmem] * len(shapes),
        compiler_params=pltpu.CompilerParams(vmem_limit_bytes=VMEM_LIMIT),
        cost_estimate=pl.CostEstimate(flops=flops, bytes_accessed=0, transcendentals=0),
    )(*held)


FIELD = (6, 16, 256)
SENT = [FIELD, (6, 8, 256), (6, 8, 256), (16, 256), (16, 256), (8, 128)]


def wall_masks(partner, codes):
    wall = jnp.repeat(partner < 0, 8)
    stuck = wall & (codes.reshape(16) == 0)
    rows = jnp.stack([jnp.where(stuck, 0.0, 1.0), jnp.where(wall, 0.0, 1.0), jnp.where(wall, 0.0, 1.0)])
    return jnp.broadcast_to(rows[:, :, None], (3, 16, 128)).astype(F32)


def pairs(count, start):
    found = []
    for i in range(start, count - 1, 2):
        found += [(i, i + 1), (i + 1, i)]
    return found


def exchange(sent):
    chord_even, chord_odd, span_even, span_odd, cut = sent
    chords, spans = lax.axis_size("chord"), lax.axis_size("span")
    cut = lax.ppermute(cut, "chord", [(i, chords - 1 - i) for i in range(chords)])
    chord_odd = lax.ppermute(chord_odd, "chord", pairs(chords, 1))
    span_odd = lax.ppermute(span_odd, "span", pairs(spans, 1))
    chord_even = lax.ppermute(chord_even, "chord", pairs(chords, 0))
    span_even = lax.ppermute(span_even, "span", pairs(spans, 0))
    return chord_even, chord_odd, span_even, span_odd, cut


def per_device(adjoint, source, diag_block, couplings, line_inverse, partner, codes):
    adjoint = adjoint.reshape(FIELD)
    source = source.reshape(FIELD)
    diag_block = diag_block.reshape(6, 6, 16, 256)
    couplings = couplings.reshape(6, 6, 6, 16, 256)
    line_inverse = line_inverse.reshape(6, 6, 2, 16, 256)
    masks = wall_masks(partner, codes)
    part, *sent = call(first_kernel, "first_edges", (source, couplings, adjoint), SENT, 5_000_000)
    for sweep in range(SWEEPS):
        got = exchange(sent)
        [part] = call(inside_kernel, "inside", (part, diag_block, couplings, adjoint), [FIELD], 4_000_000)
        arguments = (part, *got, masks, line_inverse, adjoint)
        if sweep < SWEEPS - 1:
            adjoint, part, *sent = call(
                middle_kernel, "sweep", (*arguments, source, couplings), [FIELD, *SENT], 8_000_000
            )
        else:
            adjoint, residual = call(last_kernel, "last", arguments, [FIELD, FIELD], 3_000_000, False)
    return adjoint.reshape(6, 2, 8, 256), residual.reshape(6, 2, 8, 256)


def solution(mesh):
    placed = (
        P(None, "chord", "span", None),
        P(None, "chord", "span", None),
        P(None, None, "chord", "span", None),
        P(None, None, None, "chord", "span", None),
        P(None, None, None, "chord", "span", None),
        P("chord"),
        P("chord", "span"),
    )
    return jax.shard_map(
        per_device,
        mesh=mesh,
        in_specs=placed,
        out_specs=(P(None, "chord", "span", None), P(None, "chord", "span", None)),
        check_vma=False,
    )
```

```python
import jax
import jax.numpy as jnp
from jax import lax
from jax.experimental import pallas as pl
from jax.experimental.pallas import tpu as pltpu
from jax.sharding import PartitionSpec as P

SWEEPS = 6
F32 = jnp.float32
VMEM_LIMIT = 24 * 2**20


def product(blocks, lead, field):
    out = [None] * 6
    for a in range(6):
        for b in range(6):
            term = blocks[(*lead, a, b)].astype(F32) * field[a]
            out[b] = term if a == 0 else out[b] + term
    return out


def product_rows(blocks, lead, field, low):
    out = [None] * 6
    for a in range(6):
        for b in range(6):
            term = blocks[(*lead, a, b)].astype(F32)[low : low + 8] * field[a][low : low + 8]
            out[b] = term if a == 0 else out[b] + term
    return out


def product_lanes(blocks, lead, field):
    out = [None] * 6
    for a in range(6):
        for b in range(6):
            term = blocks[(*lead, a, b, slice(None), slice(0, 128))].astype(F32) * field[a][:, 0:128]
            out[b] = term if a == 0 else out[b] + term
    return out


def inner(axis):
    index = lax.axis_index(axis)
    return (index > 0) & (index < lax.axis_size(axis) - 1)


def iotas(shape):
    return lax.broadcasted_iota(jnp.int32, shape, 0), lax.broadcasted_iota(jnp.int32, shape, 1)


def first_out(couplings, field, even_chord, out):
    cut_ref, chord_odd_ref, chord_even_ref = out
    normal = product_lanes(couplings, (4,), field)
    cut_lane = iotas((8, 128))[1]
    cut = jnp.zeros((8, 128), F32)
    for b in range(6):
        for c in range(2):
            column = normal[b][8 * c : 8 * c + 8, 0:1]
            cut = jnp.where(cut_lane == 2 * b + c, column, cut)
    cut_ref[...] = cut
    inner_chord = inner("chord")
    up = product_rows(couplings, (1,), field, 8)
    down = product_rows(couplings, (0,), field, 0)
    for b in range(6):
        chord_odd_ref[b] = jnp.where(inner_chord, jnp.where(even_chord, down[b], up[b]), 0.0)
        chord_even_ref[b] = jnp.where(even_chord, up[b], down[b])


def edges_kernel(adjoint, source, couplings, held_ref, part_ref, chord_even_ref, span_odd_ref, span_even_ref):
    even_span = lax.axis_index("span") % 2 == 0
    chord_even_ref[...] = held_ref[...]
    inner_span = inner("span")
    field = [adjoint[a] for a in range(6)]
    plus = product(couplings, (3,), field)
    minus = product(couplings, (2,), field)
    for b in range(6):
        for c in range(2):
            top, bottom = (minus[b][8 * c : 8 * c + 1], plus[b][8 * c + 7 : 8 * c + 8])
            at = 2 * b + c
            span_odd_ref[at : at + 1] = jnp.where(inner_span, jnp.where(even_span, top, bottom), 0.0)
            span_even_ref[at : at + 1] = jnp.where(even_span, bottom, top)
    row, lane = iotas((16, 256))
    row = row % 8
    for b in range(6):
        inside = jnp.where(row == 0, 0.0, pltpu.roll(plus[b], 1, 0))
        inside = inside + jnp.where(row == 7, 0.0, pltpu.roll(minus[b], 15, 0))
        part_ref[b] = source[b] - inside


def load_kernel(source, couplings, diag_block, line_inverse, adjoint, *out):
    *held, cut_ref, chord_odd_ref, chord_even_ref, sems = out
    held_adjoint, held_couplings, held_source, held_diag, held_line = held
    order = [(4, 5), (0, 2), (2, 4), (5, 6)]
    copies = [pltpu.make_async_copy(adjoint, held_adjoint, sems.at[0])]
    for i, (low, high) in enumerate(order):
        part = pl.ds(low, high - low)
        copies.append(pltpu.make_async_copy(couplings.at[part], held_couplings.at[part], sems.at[1 + i]))
    copies.append(pltpu.make_async_copy(source, held_source, sems.at[5]))
    copies.append(pltpu.make_async_copy(diag_block, held_diag, sems.at[6]))
    copies.append(pltpu.make_async_copy(line_inverse, held_line, sems.at[7]))
    for copy in copies:
        copy.start()
    for copy in copies[:3]:
        copy.wait()
    even_chord = lax.axis_index("chord") % 2 == 0
    field = [held_adjoint[a] for a in range(6)]
    first_out(held_couplings, field, even_chord, (cut_ref, chord_odd_ref, chord_even_ref))
    for copy in copies[3:]:
        copy.wait()


def inside_kernel(part, diag_block, couplings, adjoint, out):
    field = [adjoint[a] for a in range(6)]
    own = product(diag_block, (), field)
    up = product_rows(couplings, (1,), field, 0)
    down = product_rows(couplings, (0,), field, 8)
    plus = product(couplings, (5,), field)
    minus = product(couplings, (4,), field)
    lane = iotas((16, 256))[1]
    for b in range(6):
        inside = own[b] + jnp.where(lane == 0, 0.0, pltpu.roll(plus[b], 1, 1))
        inside = inside + jnp.where(lane == 255, 0.0, pltpu.roll(minus[b], 255, 1))
        inside = inside + jnp.concatenate([down[b], up[b]], axis=0)
        out[b] = part[b] - inside


def finish(part, got, masks, line_inverse, adjoint, even_chord, even_span):
    cut, chord_odd, chord_even, span_odd, span_even = got
    row, lane = iotas((16, 256))
    row = row % 8
    top = jnp.where(even_span, span_odd[...], span_even[0:16])
    bottom = jnp.where(even_span, span_even[0:16], span_odd[...])
    arrived = cut[...]
    wake = masks[2][:, 0:1] > 0
    odd_lane = lane % 2 == 1
    residual, even_part, odd_part = [], [], []
    for b in range(6):
        ev, od = chord_even[b], chord_odd[b]
        outside = jnp.concatenate([jnp.where(even_chord, od, ev), jnp.where(even_chord, ev, od)], axis=0)
        tops = jnp.concatenate(
            [jnp.broadcast_to(top[2 * b + c : 2 * b + c + 1], (8, 256)) for c in range(2)], axis=0
        )
        bottoms = jnp.concatenate(
            [jnp.broadcast_to(bottom[2 * b + c : 2 * b + c + 1], (8, 256)) for c in range(2)], axis=0
        )
        outside = outside + jnp.where(row == 0, tops, jnp.where(row == 7, bottoms, 0.0))
        columns = jnp.concatenate([arrived[:, 2 * b + 1 : 2 * b + 2], arrived[:, 2 * b : 2 * b + 1]], axis=0)
        outside = outside + jnp.where((lane == 0) & wake, columns, 0.0)
        value = part[b] - outside
        if 1 <= b <= 3:
            value = value * jnp.where(lane == 0, masks[0][:, 0:1], 1.0)
        if b == 5:
            value = value * jnp.where(lane == 0, masks[1][:, 0:1], 1.0)
        residual.append(value)
        even_part.append(jnp.where(odd_lane, pltpu.roll(value, 1, 1), value))
        odd_part.append(jnp.where(odd_lane, value, pltpu.roll(value, 255, 1)))
    after = []
    for a in range(6):
        total = adjoint[a]
        for b in range(6):
            total = total + line_inverse[a, b, 0].astype(F32) * even_part[b]
            total = total + line_inverse[a, b, 1].astype(F32) * odd_part[b]
        after.append(total)
    return residual, after


def middle_kernel(
    part, cut, chord_odd, chord_even, span_odd, span_even, masks, line_inverse, adjoint, couplings, after_ref, *out
):
    even_chord = lax.axis_index("chord") % 2 == 0
    even_span = lax.axis_index("span") % 2 == 0
    got = (cut, chord_odd, chord_even, span_odd, span_even)
    _, after = finish(part, got, masks, line_inverse, adjoint, even_chord, even_span)
    for a in range(6):
        after_ref[a] = after[a]
    first_out(couplings, after, even_chord, out)


def last_kernel(
    part, cut, chord_odd, chord_even, span_odd, span_even, masks, line_inverse, adjoint, after_ref, residual_ref
):
    even_chord = lax.axis_index("chord") % 2 == 0
    even_span = lax.axis_index("span") % 2 == 0
    got = (cut, chord_odd, chord_even, span_odd, span_even)
    residual, after = finish(part, got, masks, line_inverse, adjoint, even_chord, even_span)
    for a in range(6):
        after_ref[a] = after[a]
        residual_ref[a] = residual[a]


def call(kernel, name, operands, shapes, flops, in_vmem=True):
    vmem = pl.BlockSpec(memory_space=pltpu.VMEM)
    made = [pltpu.VMEM(s, F32) if in_vmem else jax.ShapeDtypeStruct(s, F32) for s in shapes]
    held = [pltpu.with_memory_space_constraint(x, pltpu.VMEM) for x in operands]
    return pl.pallas_call(
        kernel,
        name=name,
        out_shape=made,
        in_specs=[vmem] * len(held),
        out_specs=[vmem] * len(shapes),
        compiler_params=pltpu.CompilerParams(vmem_limit_bytes=VMEM_LIMIT),
        cost_estimate=pl.CostEstimate(flops=flops, bytes_accessed=0, transcendentals=0),
    )(*held)


FIELD = (6, 16, 256)
SLAB = (6, 8, 256)
ROWS = (16, 256)
FIRST = [(8, 128), SLAB, SLAB]
SECOND = [FIELD, SLAB, ROWS, (56, 256)]


def load(source, couplings, diag_block, line_inverse, adjoint):
    vmem = pl.BlockSpec(memory_space=pltpu.VMEM)
    operands = [
        pltpu.with_memory_space_constraint(x, pltpu.HBM) for x in (source, couplings, diag_block, line_inverse, adjoint)
    ]
    held = [pltpu.VMEM(x.shape, x.dtype) for x in (adjoint, couplings, source, diag_block, line_inverse)]
    return pl.pallas_call(
        load_kernel,
        name="load",
        out_shape=[*held, *(pltpu.VMEM(s, F32) for s in FIRST)],
        in_specs=[pl.BlockSpec(memory_space=pltpu.HBM)] * 5,
        out_specs=[vmem] * 8,
        scratch_shapes=[pltpu.SemaphoreType.DMA((8,))],
        compiler_params=pltpu.CompilerParams(vmem_limit_bytes=VMEM_LIMIT),
        cost_estimate=pl.CostEstimate(flops=1_000_000, bytes_accessed=0, transcendentals=0),
    )(*operands)


def wall_masks(partner, codes):
    wall = jnp.repeat(partner < 0, 8)
    stuck = wall & (codes.reshape(16) == 0)
    rows = jnp.stack([jnp.where(stuck, 0.0, 1.0), jnp.where(wall, 0.0, 1.0), jnp.where(wall, 0.0, 1.0)])
    return jnp.broadcast_to(rows[:, :, None], (3, 16, 128)).astype(F32)


def pairs(count, start):
    found = []
    for i in range(start, count - 1, 2):
        found += [(i, i + 1), (i + 1, i)]
    if start:
        found += [(0, count - 1), (count - 1, 0)]
    return found


def exchange(sent):
    cut, chord_odd, chord_even, span_odd, span_even = sent
    chords, spans = lax.axis_size("chord"), lax.axis_size("span")
    cut = lax.ppermute(cut, "chord", [(i, chords - 1 - i) for i in range(chords)])
    chord_odd = lax.ppermute(chord_odd, "chord", pairs(chords, 1))
    chord_even = lax.ppermute(chord_even, "chord", pairs(chords, 0))
    span_odd = lax.ppermute(span_odd, "span", pairs(spans, 1))
    span_even = lax.ppermute(span_even, "span", pairs(spans, 0))
    return cut, chord_odd, chord_even, span_odd, span_even


def per_device(adjoint, source, diag_block, couplings, line_inverse, partner, codes):
    adjoint = adjoint.reshape(FIELD)
    source = source.reshape(FIELD)
    diag_block = diag_block.reshape(6, 6, 16, 256)
    couplings = couplings.reshape(6, 6, 6, 16, 256)
    line_inverse = line_inverse.reshape(6, 6, 2, 16, 256)
    masks = wall_masks(partner, codes)
    adjoint, couplings, source, diag_block, line_inverse, *far = load(
        source, couplings, diag_block, line_inverse, adjoint
    )
    for sweep in range(SWEEPS):
        cut, chord_odd, held = far
        part, *near = call(edges_kernel, "edges", (adjoint, source, couplings, held), SECOND, 1_000)
        got = exchange((cut, chord_odd, *near))
        [part] = call(inside_kernel, "inside", (part, diag_block, couplings, adjoint), [FIELD], 20_000_000_000)
        arguments = (part, *got, masks, line_inverse, adjoint)
        if sweep < SWEEPS - 1:
            adjoint, *far = call(middle_kernel, "sweep", (*arguments, couplings), [FIELD, *FIRST], 1_000)
        else:
            adjoint, residual = call(last_kernel, "last", arguments, [FIELD, FIELD], 1_000, False)
    return adjoint.reshape(6, 2, 8, 256), residual.reshape(6, 2, 8, 256)


def solution(mesh):
    placed = (
        P(None, "chord", "span", None),
        P(None, "chord", "span", None),
        P(None, None, "chord", "span", None),
        P(None, None, None, "chord", "span", None),
        P(None, None, None, "chord", "span", None),
        P("chord"),
        P("chord", "span"),
    )
    return jax.shard_map(
        per_device,
        mesh=mesh,
        in_specs=placed,
        out_specs=(P(None, "chord", "span", None), P(None, "chord", "span", None)),
        check_vma=False,
    )
```

```python
import jax
import jax.numpy as jnp
from jax import lax
from jax.experimental import pallas as pl
from jax.experimental.pallas import tpu as pltpu
from jax.sharding import PartitionSpec as P

SWEEPS = 6
F32 = jnp.float32
VMEM_LIMIT = 24 * 2**20
INSIDE = 400_000_000


def product(blocks, lead, field):
    out = [None] * 6
    for a in range(6):
        for b in range(6):
            term = blocks[(*lead, a, b)].astype(F32) * field[a]
            out[b] = term if a == 0 else out[b] + term
    return out


def product_rows(blocks, lead, field, low):
    out = [None] * 6
    for a in range(6):
        for b in range(6):
            term = blocks[(*lead, a, b)].astype(F32)[low : low + 8] * field[a][low : low + 8]
            out[b] = term if a == 0 else out[b] + term
    return out


def product_lanes(blocks, lead, field):
    out = [None] * 6
    for a in range(6):
        for b in range(6):
            term = blocks[(*lead, a, b, slice(None), slice(0, 128))].astype(F32) * field[a][:, 0:128]
            out[b] = term if a == 0 else out[b] + term
    return out


def inner(axis):
    index = lax.axis_index(axis)
    return (index > 0) & (index < lax.axis_size(axis) - 1)


def iotas(shape):
    return lax.broadcasted_iota(jnp.int32, shape, 0), lax.broadcasted_iota(jnp.int32, shape, 1)


def first_out(couplings, field, even_chord, out):
    cut_ref, chord_odd_ref, chord_even_ref = out
    inner_chord = inner("chord")
    normal = product_lanes(couplings, (4,), field)
    cut_lane = iotas((8, 128))[1]
    cut = jnp.zeros((8, 128), F32)
    for b in range(6):
        for c in range(2):
            column = normal[b][8 * c : 8 * c + 8, 0:1]
            cut = jnp.where(cut_lane == 2 * b + c, column, cut)
    cut_ref[...] = cut
    up = product_rows(couplings, (1,), field, 8)
    down = product_rows(couplings, (0,), field, 0)
    for b in range(6):
        chord_odd_ref[b] = jnp.where(inner_chord, jnp.where(even_chord, down[b], up[b]), 0.0)
        chord_even_ref[b] = jnp.where(even_chord, up[b], down[b])


def edges_kernel(adjoint, source, couplings, part_ref, span_odd_ref, span_even_ref):
    even_span = lax.axis_index("span") % 2 == 0
    inner_span = inner("span")
    field = [adjoint[a] for a in range(6)]
    plus = product(couplings, (3,), field)
    minus = product(couplings, (2,), field)
    for b in range(6):
        for c in range(2):
            top, bottom = (minus[b][8 * c : 8 * c + 1], plus[b][8 * c + 7 : 8 * c + 8])
            at = 2 * b + c
            span_odd_ref[at : at + 1] = jnp.where(inner_span, jnp.where(even_span, top, bottom), 0.0)
            span_even_ref[at : at + 1] = jnp.where(even_span, bottom, top)
    row, lane = iotas((16, 256))
    row = row % 8
    for b in range(6):
        inside = jnp.where(row == 0, 0.0, pltpu.roll(plus[b], 1, 0))
        inside = inside + jnp.where(row == 7, 0.0, pltpu.roll(minus[b], 15, 0))
        part_ref[b] = source[b] - inside


def load_kernel(source, couplings, diag_block, line_inverse, adjoint, *out):
    *held, cut_ref, chord_odd_ref, chord_even_ref, sems = out
    held_adjoint, held_couplings, held_source, held_diag, held_line = held
    moved = [(adjoint, held_adjoint, slice(None))]
    moved += [(couplings, held_couplings, pl.ds(low, high - low)) for low, high in ((0, 2), (4, 5), (2, 4), (5, 6))]
    moved += [(source, held_source, slice(None)), (diag_block, held_diag, slice(None)), (line_inverse, held_line, slice(None))]
    copies = [pltpu.make_async_copy(a.at[i], b.at[i], sems.at[n]) for n, (a, b, i) in enumerate(moved)]
    for copy in copies:
        copy.start()
    for copy in copies[:3]:
        copy.wait()
    even_chord = lax.axis_index("chord") % 2 == 0
    field = [held_adjoint[a] for a in range(6)]
    first_out(held_couplings, field, even_chord, (cut_ref, chord_odd_ref, chord_even_ref))
    for copy in copies[3:]:
        copy.wait()


def inside_kernel(part, diag_block, couplings, adjoint, out):
    field = [adjoint[a] for a in range(6)]
    own = product(diag_block, (), field)
    up = product_rows(couplings, (1,), field, 0)
    down = product_rows(couplings, (0,), field, 8)
    plus = product(couplings, (5,), field)
    minus = product(couplings, (4,), field)
    lane = iotas((16, 256))[1]
    for b in range(6):
        inside = own[b] + jnp.where(lane == 0, 0.0, pltpu.roll(plus[b], 1, 1))
        inside = inside + jnp.where(lane == 255, 0.0, pltpu.roll(minus[b], 255, 1))
        inside = inside + jnp.concatenate([down[b], up[b]], axis=0)
        out[b] = part[b] - inside


def first_inside_kernel(part, diag_block, couplings, adjoint, partner, codes, out, masks_ref):
    inside_kernel(part, diag_block, couplings, adjoint, out)
    here, there = iotas((8, 8))
    for c in range(2):
        rows = jnp.broadcast_to(codes[c : c + 1, :], (8, 8))
        code = jnp.sum(jnp.where(here == there, rows, 0), axis=1, keepdims=True)
        wall = jnp.broadcast_to(partner[:, c : c + 1], (8, 1)) < 0
        factors = (
            jnp.where(wall & (code == 0), 0.0, 1.0),
            jnp.where(wall, 0.0, 1.0),
            jnp.where(wall, 0.0, 1.0),
        )
        for i, factor in enumerate(factors):
            masks_ref[i, 8 * c : 8 * c + 8, :] = jnp.broadcast_to(factor.astype(F32), (8, 128))


def sweep_residual(part, got, masks, even_chord, even_span):
    cut, chord_odd, chord_even, span_odd, span_even = got
    row, lane = iotas((16, 256))
    row = row % 8
    top = jnp.where(even_span, span_odd[...], span_even[0:16])
    bottom = jnp.where(even_span, span_even[0:16], span_odd[...])
    arrived = cut[...]
    wake = masks[2][:, 0:1] > 0
    odd_lane = lane % 2 == 1
    residual, even_part, odd_part = [], [], []
    for b in range(6):
        ev, od = chord_even[b], chord_odd[b]
        outside = jnp.concatenate([jnp.where(even_chord, od, ev), jnp.where(even_chord, ev, od)], axis=0)
        tops = jnp.concatenate(
            [jnp.broadcast_to(top[2 * b + c : 2 * b + c + 1], (8, 256)) for c in range(2)], axis=0
        )
        bottoms = jnp.concatenate(
            [jnp.broadcast_to(bottom[2 * b + c : 2 * b + c + 1], (8, 256)) for c in range(2)], axis=0
        )
        outside = outside + jnp.where(row == 0, tops, jnp.where(row == 7, bottoms, 0.0))
        columns = jnp.concatenate([arrived[:, 2 * b + 1 : 2 * b + 2], arrived[:, 2 * b : 2 * b + 1]], axis=0)
        outside = outside + jnp.where((lane == 0) & wake, columns, 0.0)
        value = part[b] - outside
        if 1 <= b <= 3:
            value = value * jnp.where(lane == 0, masks[0][:, 0:1], 1.0)
        if b == 5:
            value = value * jnp.where(lane == 0, masks[1][:, 0:1], 1.0)
        residual.append(value)
        even_part.append(jnp.where(odd_lane, pltpu.roll(value, 1, 1), value))
        odd_part.append(jnp.where(odd_lane, value, pltpu.roll(value, 255, 1)))
    return residual, (even_part, odd_part)


def line_update(line_inverse, adjoint, parts, a):
    total = adjoint[a]
    for b in range(6):
        for q in range(2):
            total = total + line_inverse[a, b, q].astype(F32) * parts[q][b]
    return total


def middle_kernel(
    part, cut, chord_odd, chord_even, span_odd, span_even, masks, line_inverse, adjoint, couplings, after_ref, *out
):
    even_chord = lax.axis_index("chord") % 2 == 0
    even_span = lax.axis_index("span") % 2 == 0
    got = (cut, chord_odd, chord_even, span_odd, span_even)
    _, parts = sweep_residual(part, got, masks, even_chord, even_span)
    after = [line_update(line_inverse, adjoint, parts, a) for a in range(6)]
    for a in range(6):
        after_ref[a] = after[a]
    first_out(couplings, after, even_chord, out)


def last_kernel(
    part, cut, chord_odd, chord_even, span_odd, span_even, masks, line_inverse, adjoint, after_ref, residual_ref,
    held_after, held_residual, sems
):
    even_chord = lax.axis_index("chord") % 2 == 0
    even_span = lax.axis_index("span") % 2 == 0
    got = (cut, chord_odd, chord_even, span_odd, span_even)
    residual, parts = sweep_residual(part, got, masks, even_chord, even_span)
    for a in range(6):
        held_residual[a] = residual[a]
    copies = [pltpu.make_async_copy(held_residual, residual_ref, sems.at[0])]
    copies[0].start()
    for half in range(2):
        for a in range(3 * half, 3 * half + 3):
            held_after[a] = line_update(line_inverse, adjoint, parts, a)
        rows = pl.ds(3 * half, 3)
        copies.append(pltpu.make_async_copy(held_after.at[rows], after_ref.at[rows], sems.at[1 + half]))
        copies[-1].start()
    for copy in copies:
        copy.wait()


def call(kernel, name, operands, shapes, flops, in_vmem=True):
    vmem = pl.BlockSpec(memory_space=pltpu.VMEM)
    space = pltpu.VMEM if in_vmem else pltpu.HBM
    held = [pltpu.with_memory_space_constraint(x, pltpu.VMEM) for x in operands]
    return pl.pallas_call(
        kernel,
        name=name,
        out_shape=[space(s, F32) for s in shapes],
        in_specs=[vmem] * len(held),
        out_specs=[pl.BlockSpec(memory_space=space)] * len(shapes),
        scratch_shapes=[] if in_vmem else [*(pltpu.VMEM(s, F32) for s in shapes), pltpu.SemaphoreType.DMA((3,))],
        compiler_params=pltpu.CompilerParams(vmem_limit_bytes=VMEM_LIMIT),
        cost_estimate=pl.CostEstimate(flops=flops, bytes_accessed=0, transcendentals=0),
    )(*held)


FIELD = (6, 16, 256)
SLAB = (6, 8, 256)
ROWS = (16, 256)
FIRST = [(8, 128), SLAB, SLAB]
SECOND = [FIELD, ROWS, (24, 256)]


def load(source, couplings, diag_block, line_inverse, adjoint):
    vmem = pl.BlockSpec(memory_space=pltpu.VMEM)
    operands = [
        pltpu.with_memory_space_constraint(x, pltpu.HBM) for x in (source, couplings, diag_block, line_inverse, adjoint)
    ]
    held = [pltpu.VMEM(x.shape, x.dtype) for x in (adjoint, couplings, source, diag_block, line_inverse)]
    return pl.pallas_call(
        load_kernel,
        name="load",
        out_shape=[*held, *(pltpu.VMEM(s, F32) for s in FIRST)],
        in_specs=[pl.BlockSpec(memory_space=pltpu.HBM)] * 5,
        out_specs=[vmem] * 8,
        scratch_shapes=[pltpu.SemaphoreType.DMA((8,))],
        compiler_params=pltpu.CompilerParams(vmem_limit_bytes=VMEM_LIMIT),
        cost_estimate=pl.CostEstimate(flops=1_000_000, bytes_accessed=0, transcendentals=0),
    )(*operands)


def pairs(chords, spans, axis, start):
    found = []
    for chord in range(chords):
        for span in range(spans):
            index, count = (chord, chords) if axis == "chord" else (span, spans)
            other = index + 1 if (index - start) % 2 == 0 else index - 1
            if 0 <= other < count:
                to = (other, span) if axis == "chord" else (chord, other)
            else:
                to = (chord, span ^ 1) if axis == "chord" else (chord ^ 1, span)
            found.append((chord * spans + span, to[0] * spans + to[1]))
    return found


def exchange(sent):
    cut, chord_odd, chord_even, span_odd, span_even = sent
    chords, spans = lax.axis_size("chord"), lax.axis_size("span")
    cut = lax.ppermute(cut, "chord", [(i, chords - 1 - i) for i in range(chords)])
    chord_odd = lax.ppermute(chord_odd, ("chord", "span"), pairs(chords, spans, "chord", 1))
    chord_even = lax.ppermute(chord_even, ("chord", "span"), pairs(chords, spans, "chord", 0))
    span_odd = lax.ppermute(span_odd, ("chord", "span"), pairs(chords, spans, "span", 1))
    span_even = lax.ppermute(span_even, ("chord", "span"), pairs(chords, spans, "span", 0))
    return cut, chord_odd, chord_even, span_odd, span_even


def per_device(adjoint, source, diag_block, couplings, line_inverse, partner, codes):
    adjoint = adjoint.reshape(FIELD)
    source = source.reshape(FIELD)
    diag_block = diag_block.reshape(6, 6, 16, 256)
    couplings = couplings.reshape(6, 6, 6, 16, 256)
    line_inverse = line_inverse.reshape(6, 6, 2, 16, 256)
    adjoint, couplings, source, diag_block, line_inverse, *far = load(
        source, couplings, diag_block, line_inverse, adjoint
    )
    for sweep in range(SWEEPS):
        part, *near = call(edges_kernel, "edges", (adjoint, source, couplings), SECOND, 1_000)
        got = exchange((*far, *near))
        held = (part, diag_block, couplings, adjoint)
        if sweep == 0:
            part, masks = call(
                first_inside_kernel, "inside_masks", (*held, partner.reshape(1, 2), codes), [FIELD, (3, 16, 128)], INSIDE
            )
        else:
            [part] = call(inside_kernel, "inside", held, [FIELD], INSIDE)
        arguments = (part, *got, masks, line_inverse, adjoint)
        if sweep < SWEEPS - 1:
            adjoint, *far = call(middle_kernel, "sweep", (*arguments, couplings), [FIELD, *FIRST], 1_000)
        else:
            adjoint, residual = call(last_kernel, "last", arguments, [FIELD, FIELD], 1_000, False)
    return adjoint.reshape(6, 2, 8, 256), residual.reshape(6, 2, 8, 256)


def solution(mesh):
    placed = (
        P(None, "chord", "span", None),
        P(None, "chord", "span", None),
        P(None, None, "chord", "span", None),
        P(None, None, None, "chord", "span", None),
        P(None, None, None, "chord", "span", None),
        P("chord"),
        P("chord", "span"),
    )
    return jax.shard_map(
        per_device,
        mesh=mesh,
        in_specs=placed,
        out_specs=(P(None, "chord", "span", None), P(None, "chord", "span", None)),
        check_vma=False,
    )
```

```python
import jax
import jax.numpy as jnp
from jax import lax
from jax.experimental import pallas as pl
from jax.experimental.pallas import tpu as pltpu
from jax.sharding import PartitionSpec as P

SWEEPS = 6
F32 = jnp.float32
VMEM_LIMIT = 24 * 2**20
SETTLE = 1_000
INSIDE = 400_000_000


def product(blocks, lead, field):
    out = [None] * 6
    for a in range(6):
        for b in range(6):
            term = blocks[(*lead, a, b)].astype(F32) * field[a]
            out[b] = term if a == 0 else out[b] + term
    return out


def product_rows(blocks, lead, field, low, lanes=256):
    out = [None] * 6
    for a in range(6):
        for b in range(6):
            block = blocks[(*lead, a, b, slice(None), slice(0, lanes))].astype(F32)
            term = block[low : low + 8] * field[a][low : low + 8]
            out[b] = term if a == 0 else out[b] + term
    return out


def product_lanes(blocks, lead, field):
    out = [None] * 6
    for a in range(6):
        for b in range(6):
            term = blocks[(*lead, a, b, slice(None), slice(0, 128))].astype(F32) * field[a][:, 0:128]
            out[b] = term if a == 0 else out[b] + term
    return out


def inner(axis):
    index = lax.axis_index(axis)
    return (index > 0) & (index < lax.axis_size(axis) - 1)


def beside_mirror():
    half = lax.axis_size("chord") // 2
    index = lax.axis_index("chord")
    return (index == half - 1) | (index == half)


def iotas(shape):
    return lax.broadcasted_iota(jnp.int32, shape, 0), lax.broadcasted_iota(jnp.int32, shape, 1)


def cut_row(couplings, field):
    normal = product_lanes(couplings, (4,), field)
    lane = iotas((8, 128))[1]
    row = jnp.zeros((8, 128), F32)
    for b in range(6):
        for c in range(2):
            column = normal[b][8 * c : 8 * c + 8, 0:1]
            row = jnp.where(lane // 2 == 2 * b + c, column, row)
    return row


def chord_products(up, down, odd_ref, even_ref):
    even_chord = lax.axis_index("chord") % 2 == 0
    inner_chord = inner("chord")
    for b in range(6):
        odd_ref[b] = jnp.where(inner_chord, jnp.where(even_chord, down[b], up[b]), 0.0)
        even_ref[b] = jnp.where(even_chord, up[b], down[b])


def first_out(couplings, field, out):
    cut_ref, chord_odd_ref, chord_even_ref = out
    row = cut_row(couplings, field)
    cut_ref[...] = row
    chord_odd_ref[6, :, 0:128] = row
    up = product_rows(couplings, (1,), field, 8)
    down = product_rows(couplings, (0,), field, 0)
    chord_products(up, down, chord_odd_ref, chord_even_ref)


def edges_kernel(adjoint, source, couplings, part_ref, span_odd_ref, span_even_ref):
    even_span = lax.axis_index("span") % 2 == 0
    inner_span = inner("span")
    field = [adjoint[a] for a in range(6)]
    plus = product(couplings, (3,), field)
    minus = product(couplings, (2,), field)
    for b in range(6):
        for c in range(2):
            top, bottom = (minus[b][8 * c : 8 * c + 1], plus[b][8 * c + 7 : 8 * c + 8])
            at = 2 * b + c
            span_odd_ref[at : at + 1] = jnp.where(inner_span, jnp.where(even_span, top, bottom), 0.0)
            span_even_ref[at : at + 1] = jnp.where(even_span, bottom, top)
    row, lane = iotas((16, 256))
    row = row % 8
    for b in range(6):
        inside = jnp.where(row == 0, 0.0, pltpu.roll(plus[b], 1, 0))
        inside = inside + jnp.where(row == 7, 0.0, pltpu.roll(minus[b], 15, 0))
        part_ref[b] = source[b] - inside


def load_kernel(couplings, adjoint, *out):
    *held, cut_ref, chord_odd_ref, chord_even_ref, sems = out
    held_adjoint, held_couplings = held
    moved = [(adjoint, held_adjoint, slice(None))]
    moved += [(couplings, held_couplings, pl.ds(low, high - low)) for low, high in ((0, 2), (4, 5), (2, 4), (5, 6))]
    copies = [pltpu.make_async_copy(a.at[i], b.at[i], sems.at[n]) for n, (a, b, i) in enumerate(moved)]
    for copy in copies:
        copy.start()
    for copy in copies[:3]:
        copy.wait()
    field = [held_adjoint[a] for a in range(6)]
    first_out(held_couplings, field, (cut_ref, chord_odd_ref, chord_even_ref))
    for copy in copies[3:]:
        copy.wait()


def inside_kernel(part, diag_block, couplings, adjoint, out):
    field = [adjoint[a] for a in range(6)]
    own = product(diag_block, (), field)
    up = product_rows(couplings, (1,), field, 0)
    down = product_rows(couplings, (0,), field, 8)
    plus = product(couplings, (5,), field)
    minus = product(couplings, (4,), field)
    lane = iotas((16, 256))[1]
    for b in range(6):
        inside = own[b] + jnp.where(lane == 0, 0.0, pltpu.roll(plus[b], 1, 1))
        inside = inside + jnp.where(lane == 255, 0.0, pltpu.roll(minus[b], 255, 1))
        inside = inside + jnp.concatenate([down[b], up[b]], axis=0)
        out[b] = part[b] - inside


def first_inside_kernel(part, diag_block, couplings, adjoint, partner, codes, out, masks_ref):
    inside_kernel(part, diag_block, couplings, adjoint, out)
    here, there = iotas((8, 8))
    for c in range(2):
        rows = jnp.broadcast_to(codes[c : c + 1, :], (8, 8))
        code = jnp.sum(jnp.where(here == there, rows, 0), axis=1, keepdims=True)
        wall = jnp.broadcast_to(partner[:, c : c + 1], (8, 1)) < 0
        factors = (
            jnp.where(wall & (code == 0), 0.0, 1.0),
            jnp.where(wall, 0.0, 1.0),
            jnp.where(wall, 0.0, 1.0),
        )
        for i, factor in enumerate(factors):
            masks_ref[i, 8 * c : 8 * c + 8, :] = jnp.broadcast_to(factor.astype(F32), (8, 128))


def sweep_residual(part, got, masks, even_chord, even_span):
    chord_odd, chord_even, span_odd, span_even = got
    row, lane = iotas((16, 256))
    row = row % 8
    top = jnp.where(even_span, span_odd[...], span_even[0:16])
    bottom = jnp.where(even_span, span_even[0:16], span_odd[...])
    odd_lane = lane % 2 == 1
    residual, even_part, odd_part = [], [], []
    for b in range(6):
        ev, od = chord_even[b], chord_odd[b]
        outside = jnp.concatenate([jnp.where(even_chord, od, ev), jnp.where(even_chord, ev, od)], axis=0)
        tops = jnp.concatenate(
            [jnp.broadcast_to(top[2 * b + c : 2 * b + c + 1], (8, 256)) for c in range(2)], axis=0
        )
        bottoms = jnp.concatenate(
            [jnp.broadcast_to(bottom[2 * b + c : 2 * b + c + 1], (8, 256)) for c in range(2)], axis=0
        )
        outside = outside + jnp.where(row == 0, tops, jnp.where(row == 7, bottoms, 0.0))
        value = part[b] - outside
        if 1 <= b <= 3:
            value = value * jnp.where(lane == 0, masks[0][:, 0:1], 1.0)
        if b == 5:
            value = value * jnp.where(lane == 0, masks[1][:, 0:1], 1.0)
        residual.append(value)
        even_part.append(jnp.where(odd_lane, pltpu.roll(value, 1, 1), value))
        odd_part.append(jnp.where(odd_lane, value, pltpu.roll(value, 255, 1)))
    return residual, (even_part, odd_part)


def line_update(line_inverse, adjoint, parts, a):
    total = adjoint[a]
    for b in range(6):
        for q in range(2):
            total = total + line_inverse[a, b, q].astype(F32) * parts[q][b]
    return total


def settle(part, got, masks, line_inverse, adjoint):
    even_chord = lax.axis_index("chord") % 2 == 0
    even_span = lax.axis_index("span") % 2 == 0
    residual, parts = sweep_residual(part, got, masks, even_chord, even_span)
    return residual, [line_update(line_inverse, adjoint, parts, a) for a in range(6)]


def settle_kernel(
    part, chord_odd, chord_even, span_odd, span_even, masks, line_inverse, adjoint, couplings, after_ref, odd_ref, even_ref
):
    _, after = settle(part, (chord_odd, chord_even, span_odd, span_even), masks, line_inverse, adjoint)
    for a in range(6):
        after_ref[a] = after[a]
    up = product_rows(couplings, (1,), after, 8)
    down = product_rows(couplings, (0,), after, 0)
    chord_products(up, down, odd_ref, even_ref)


def last_settle_kernel(
    part, chord_odd, chord_even, span_odd, span_even, masks, line_inverse, adjoint, after_ref, residual_ref
):
    residual, after = settle(part, (chord_odd, chord_even, span_odd, span_even), masks, line_inverse, adjoint)
    for a in range(6):
        after_ref[a] = after[a]
        residual_ref[a] = residual[a]


def cut_change(cut, chord_odd, masks, line_inverse):
    arrived = jnp.where(beside_mirror(), chord_odd[6, :, 0:128], cut[...])
    wake = masks[2] > 0
    lane = iotas((16, 128))[1]
    columns = []
    for b in range(6):
        slabs = [pltpu.roll(arrived, (128 - 4 * b - 2 * c) % 128, 1) for c in (1, 0)]
        columns.append(jnp.where(wake, -jnp.concatenate(slabs, axis=0), 0.0))
    change = [jnp.where(lane == 0, column, 0.0) for column in columns]
    delta = []
    for a in range(6):
        total = None
        for b in range(6):
            term = line_inverse[a, b, 0, :, 0:128].astype(F32) * columns[b]
            total = term if b == 0 else total + term
        delta.append(jnp.where(lane < 2, total, 0.0))
    return change, delta


def cut_kernel(
    cut, chord_odd, masks, line_inverse, couplings, main, odd, even, after_ref, cut_ref, chord_odd_ref, chord_even_ref
):
    _, delta = cut_change(cut, chord_odd, masks, line_inverse)
    near = [main[a, :, 0:128] + delta[a] for a in range(6)]
    for a in range(6):
        after_ref[a, :, 0:128] = near[a]
        after_ref[a, :, 128:256] = main[a, :, 128:256]
    row = cut_row(couplings, near)
    cut_ref[...] = row
    chord_odd_ref[6, :, 0:128] = row
    chord_odd_ref[0:6] = odd[...]
    chord_even_ref[...] = even[...]
    up = product_rows(couplings, (1,), delta, 8, 128)
    down = product_rows(couplings, (0,), delta, 0, 128)
    even_chord = lax.axis_index("chord") % 2 == 0
    inner_chord = inner("chord")
    for b in range(6):
        first = jnp.where(inner_chord, jnp.where(even_chord, down[b], up[b]), 0.0)
        chord_odd_ref[b, :, 0:128] = odd[b, :, 0:128] + first
        chord_even_ref[b, :, 0:128] = even[b, :, 0:128] + jnp.where(even_chord, up[b], down[b])


def last_cut_kernel(
    cut, chord_odd, masks, line_inverse, main, held, after_ref, residual_ref, after_scratch, residual_scratch, sems
):
    change, delta = cut_change(cut, chord_odd, masks, line_inverse)
    copies = []
    for i, (old, added, scratch, to) in enumerate(
        ((held, change, residual_scratch, residual_ref), (main, delta, after_scratch, after_ref))
    ):
        for a in range(6):
            scratch[a, :, 0:128] = old[a, :, 0:128] + added[a]
            scratch[a, :, 128:256] = old[a, :, 128:256]
        copies.append(pltpu.make_async_copy(scratch, to, sems.at[i]))
        copies[-1].start()
    for copy in copies:
        copy.wait()


def call(kernel, name, operands, shapes, flops, in_vmem=True):
    vmem = pl.BlockSpec(memory_space=pltpu.VMEM)
    space = pltpu.VMEM if in_vmem else pltpu.HBM
    held = [pltpu.with_memory_space_constraint(x, pltpu.VMEM) for x in operands]
    return pl.pallas_call(
        kernel,
        name=name,
        out_shape=[space(s, F32) for s in shapes],
        in_specs=[vmem] * len(held),
        out_specs=[pl.BlockSpec(memory_space=space)] * len(shapes),
        scratch_shapes=[] if in_vmem else [*(pltpu.VMEM(s, F32) for s in shapes), pltpu.SemaphoreType.DMA((2,))],
        compiler_params=pltpu.CompilerParams(vmem_limit_bytes=VMEM_LIMIT),
        cost_estimate=pl.CostEstimate(flops=flops, bytes_accessed=0, transcendentals=0),
    )(*held)


FIELD = (6, 16, 256)
SLAB = (6, 8, 256)
ROWS = (16, 256)
FIRST = [(8, 128), (7, 8, 256), SLAB]
SECOND = [FIELD, ROWS, (24, 256)]


def load(couplings, adjoint):
    vmem = pl.BlockSpec(memory_space=pltpu.VMEM)
    operands = [
        pltpu.with_memory_space_constraint(x, pltpu.HBM) for x in (couplings, adjoint)
    ]
    held = [pltpu.VMEM(x.shape, x.dtype) for x in (adjoint, couplings)]
    return pl.pallas_call(
        load_kernel,
        name="load",
        out_shape=[*held, *(pltpu.VMEM(s, F32) for s in FIRST)],
        in_specs=[pl.BlockSpec(memory_space=pltpu.HBM)] * 2,
        out_specs=[vmem] * 5,
        scratch_shapes=[pltpu.SemaphoreType.DMA((5,))],
        compiler_params=pltpu.CompilerParams(vmem_limit_bytes=VMEM_LIMIT),
        cost_estimate=pl.CostEstimate(flops=1_000_000, bytes_accessed=0, transcendentals=0),
    )(*operands)


def pairs(chords, spans, axis, start):
    found = []
    for chord in range(chords):
        for span in range(spans):
            index, count = (chord, chords) if axis == "chord" else (span, spans)
            other = index + 1 if (index - start) % 2 == 0 else index - 1
            if 0 <= other < count:
                to = (other, span) if axis == "chord" else (chord, other)
            else:
                to = (chord, span ^ 1) if axis == "chord" else (chord ^ 1, span)
            found.append((chord * spans + span, to[0] * spans + to[1]))
    return found


def mirrors(chords, spans):
    found = []
    for chord in range(chords):
        for span in range(spans):
            if abs(2 * chord + 1 - chords) == 1:
                to = (chord, span ^ 1)
            else:
                to = (chords - 1 - chord, span)
            found.append((chord * spans + span, to[0] * spans + to[1]))
    return found


def exchange(sent):
    cut, chord_odd, chord_even, span_odd, span_even = sent
    chords, spans = lax.axis_size("chord"), lax.axis_size("span")
    cut = lax.ppermute(cut, ("chord", "span"), mirrors(chords, spans))
    chord_odd = lax.ppermute(chord_odd, ("chord", "span"), pairs(chords, spans, "chord", 1))
    chord_even = lax.ppermute(chord_even, ("chord", "span"), pairs(chords, spans, "chord", 0))
    span_odd = lax.ppermute(span_odd, ("chord", "span"), pairs(chords, spans, "span", 1))
    span_even = lax.ppermute(span_even, ("chord", "span"), pairs(chords, spans, "span", 0))
    return cut, chord_odd, chord_even, span_odd, span_even


def per_device(adjoint, source, diag_block, couplings, line_inverse, partner, codes):
    adjoint = adjoint.reshape(FIELD)
    source = source.reshape(FIELD)
    diag_block = diag_block.reshape(6, 6, 16, 256)
    couplings = couplings.reshape(6, 6, 6, 16, 256)
    line_inverse = line_inverse.reshape(6, 6, 2, 16, 256)
    adjoint, couplings, *far = load(couplings, adjoint)
    for sweep in range(SWEEPS):
        part, *near = call(edges_kernel, "edges", (adjoint, source, couplings), SECOND, 1_000)
        got = exchange((*far, *near))
        held = (part, diag_block, couplings, adjoint)
        if sweep == 0:
            part, masks = call(
                first_inside_kernel, "inside_masks", (*held, partner.reshape(1, 2), codes), [FIELD, (3, 16, 128)], INSIDE
            )
        else:
            [part] = call(inside_kernel, "inside", held, [FIELD], INSIDE)
        cut, *beside = got
        arguments = (part, *beside, masks, line_inverse, adjoint)
        late = (cut, beside[0], masks, line_inverse)
        if sweep < SWEEPS - 1:
            main, odd, even = call(settle_kernel, "settle", (*arguments, couplings), [FIELD, SLAB, SLAB], SETTLE)
            adjoint, *far = call(cut_kernel, "cut", (*late, couplings, main, odd, even), [FIELD, *FIRST], 1_000)
        else:
            main, held = call(last_settle_kernel, "last_settle", arguments, [FIELD, FIELD], SETTLE)
            adjoint, residual = call(last_cut_kernel, "last", (*late, main, held), [FIELD, FIELD], 1_000, False)
    return adjoint.reshape(6, 2, 8, 256), residual.reshape(6, 2, 8, 256)


def solution(mesh):
    placed = (
        P(None, "chord", "span", None),
        P(None, "chord", "span", None),
        P(None, None, "chord", "span", None),
        P(None, None, None, "chord", "span", None),
        P(None, None, None, "chord", "span", None),
        P("chord"),
        P("chord", "span"),
    )
    return jax.shard_map(
        per_device,
        mesh=mesh,
        in_specs=placed,
        out_specs=(P(None, "chord", "span", None), P(None, "chord", "span", None)),
        check_vma=False,
    )
```

```python
import jax
import jax.numpy as jnp
from jax import lax
from jax.experimental import pallas as pl
from jax.experimental.pallas import tpu as pltpu
from jax.sharding import PartitionSpec as P

SWEEPS = 6
F32 = jnp.float32
VMEM_LIMIT = 24 * 2**20
SETTLE = 1_000
INSIDE = 400_000_000


def product(blocks, lead, field):
    out = [None] * 6
    for a in range(6):
        for b in range(6):
            term = blocks[(*lead, a, b)].astype(F32) * field[a]
            out[b] = term if a == 0 else out[b] + term
    return out


def product_rows(blocks, lead, field, low, lanes=256):
    out = [None] * 6
    for a in range(6):
        for b in range(6):
            block = blocks[(*lead, a, b, slice(None), slice(0, lanes))].astype(F32)
            term = block[low : low + 8] * field[a][low : low + 8]
            out[b] = term if a == 0 else out[b] + term
    return out


def product_lanes(blocks, lead, field):
    out = [None] * 6
    for a in range(6):
        for b in range(6):
            term = blocks[(*lead, a, b, slice(None), slice(0, 128))].astype(F32) * field[a][:, 0:128]
            out[b] = term if a == 0 else out[b] + term
    return out


def inner(axis):
    index = lax.axis_index(axis)
    return (index > 0) & (index < lax.axis_size(axis) - 1)


def beside_mirror():
    half = lax.axis_size("chord") // 2
    index = lax.axis_index("chord")
    return (index == half - 1) | (index == half)


def iotas(shape):
    return lax.broadcasted_iota(jnp.int32, shape, 0), lax.broadcasted_iota(jnp.int32, shape, 1)


def cut_row(couplings, field):
    normal = product_lanes(couplings, (4,), field)
    lane = iotas((8, 128))[1]
    row = jnp.zeros((8, 128), F32)
    for b in range(6):
        for c in range(2):
            column = normal[b][8 * c : 8 * c + 8, 0:1]
            row = jnp.where(lane // 2 == 2 * b + c, column, row)
    return row


def chord_products(up, down, odd_ref, even_ref):
    even_chord = lax.axis_index("chord") % 2 == 0
    inner_chord = inner("chord")
    for b in range(6):
        odd_ref[b] = jnp.where(inner_chord, jnp.where(even_chord, down[b], up[b]), 0.0)
        even_ref[b] = jnp.where(even_chord, up[b], down[b])


def first_out(couplings, field, out):
    cut_ref, chord_odd_ref, chord_even_ref = out
    row = cut_row(couplings, field)
    cut_ref[...] = row
    chord_odd_ref[6, :, 0:128] = row
    up = product_rows(couplings, (1,), field, 8)
    down = product_rows(couplings, (0,), field, 0)
    chord_products(up, down, chord_odd_ref, chord_even_ref)


def edges_kernel(adjoint, couplings, span_odd_ref, span_even_ref):
    even_span = lax.axis_index("span") % 2 == 0
    inner_span = inner("span")
    last = iotas((16, 256))[0] % 8 == 7
    made = [None] * 6
    for a in range(6):
        for b in range(6):
            block = jnp.where(last, couplings[3, a, b], couplings[2, a, b]).astype(F32)
            term = block * adjoint[a]
            made[b] = term if a == 0 else made[b] + term
    for b in range(6):
        for c in range(2):
            top, bottom = (made[b][8 * c : 8 * c + 1], made[b][8 * c + 7 : 8 * c + 8])
            at = 2 * b + c
            span_odd_ref[at : at + 1] = jnp.where(inner_span, jnp.where(even_span, top, bottom), 0.0)
            span_even_ref[at : at + 1] = jnp.where(even_span, bottom, top)


def load_kernel(couplings, adjoint, *out):
    *held, cut_ref, chord_odd_ref, chord_even_ref, sems = out
    held_adjoint, held_couplings = held
    moved = [(adjoint, held_adjoint, slice(None))]
    moved += [(couplings, held_couplings, pl.ds(low, high - low)) for low, high in ((0, 2), (4, 5), (2, 4), (5, 6))]
    copies = [pltpu.make_async_copy(a.at[i], b.at[i], sems.at[n]) for n, (a, b, i) in enumerate(moved)]
    for copy in copies:
        copy.start()
    for copy in copies[:3]:
        copy.wait()
    field = [held_adjoint[a] for a in range(6)]
    first_out(held_couplings, field, (cut_ref, chord_odd_ref, chord_even_ref))
    for copy in copies[3:]:
        copy.wait()


def inside_kernel(sent, source, diag_block, couplings, adjoint, out):
    field = [adjoint[a] for a in range(6)]
    row, lane = iotas((16, 256))
    row = row % 8
    span_plus = product(couplings, (3,), field)
    span_minus = product(couplings, (2,), field)
    for b in range(6):
        inside = jnp.where(row == 0, 0.0, pltpu.roll(span_plus[b], 1, 0))
        inside = inside + jnp.where(row == 7, 0.0, pltpu.roll(span_minus[b], 15, 0))
        out[b] = source[b] - inside
    own = product(diag_block, (), field)
    up = product_rows(couplings, (1,), field, 0)
    down = product_rows(couplings, (0,), field, 8)
    plus = product(couplings, (5,), field)
    minus = product(couplings, (4,), field)
    for b in range(6):
        inside = own[b] + jnp.where(lane == 0, 0.0, pltpu.roll(plus[b], 1, 1))
        inside = inside + jnp.where(lane == 255, 0.0, pltpu.roll(minus[b], 255, 1))
        inside = inside + jnp.concatenate([down[b], up[b]], axis=0)
        out[b] = out[b] - inside


def first_inside_kernel(sent, source, diag_block, couplings, adjoint, partner, codes, out, masks_ref):
    inside_kernel(sent, source, diag_block, couplings, adjoint, out)
    here, there = iotas((8, 8))
    for c in range(2):
        rows = jnp.broadcast_to(codes[c : c + 1, :], (8, 8))
        code = jnp.sum(jnp.where(here == there, rows, 0), axis=1, keepdims=True)
        wall = jnp.broadcast_to(partner[:, c : c + 1], (8, 1)) < 0
        factors = (
            jnp.where(wall & (code == 0), 0.0, 1.0),
            jnp.where(wall, 0.0, 1.0),
            jnp.where(wall, 0.0, 1.0),
        )
        for i, factor in enumerate(factors):
            masks_ref[i, 8 * c : 8 * c + 8, :] = jnp.broadcast_to(factor.astype(F32), (8, 128))


def sweep_residual(part, got, masks, even_chord, even_span):
    chord_odd, chord_even, span_odd, span_even = got
    row, lane = iotas((16, 256))
    row = row % 8
    top = jnp.where(even_span, span_odd[...], span_even[0:16])
    bottom = jnp.where(even_span, span_even[0:16], span_odd[...])
    odd_lane = lane % 2 == 1
    residual, even_part, odd_part = [], [], []
    for b in range(6):
        ev, od = chord_even[b], chord_odd[b]
        outside = jnp.concatenate([jnp.where(even_chord, od, ev), jnp.where(even_chord, ev, od)], axis=0)
        tops = jnp.concatenate(
            [jnp.broadcast_to(top[2 * b + c : 2 * b + c + 1], (8, 256)) for c in range(2)], axis=0
        )
        bottoms = jnp.concatenate(
            [jnp.broadcast_to(bottom[2 * b + c : 2 * b + c + 1], (8, 256)) for c in range(2)], axis=0
        )
        outside = outside + jnp.where(row == 0, tops, jnp.where(row == 7, bottoms, 0.0))
        value = part[b] - outside
        if 1 <= b <= 3:
            value = value * jnp.where(lane == 0, masks[0][:, 0:1], 1.0)
        if b == 5:
            value = value * jnp.where(lane == 0, masks[1][:, 0:1], 1.0)
        residual.append(value)
        even_part.append(jnp.where(odd_lane, pltpu.roll(value, 1, 1), value))
        odd_part.append(jnp.where(odd_lane, value, pltpu.roll(value, 255, 1)))
    return residual, (even_part, odd_part)


def line_update(line_inverse, adjoint, parts, a):
    total = adjoint[a]
    for b in range(6):
        for q in range(2):
            total = total + line_inverse[a, b, q].astype(F32) * parts[q][b]
    return total


def settle(part, got, masks, line_inverse, adjoint):
    even_chord = lax.axis_index("chord") % 2 == 0
    even_span = lax.axis_index("span") % 2 == 0
    residual, parts = sweep_residual(part, got, masks, even_chord, even_span)
    return residual, [line_update(line_inverse, adjoint, parts, a) for a in range(6)]


def settle_kernel(
    part, chord_odd, chord_even, span_odd, span_even, masks, line_inverse, adjoint, couplings, after_ref, odd_ref, even_ref
):
    _, after = settle(part, (chord_odd, chord_even, span_odd, span_even), masks, line_inverse, adjoint)
    for a in range(6):
        after_ref[a] = after[a]
    up = product_rows(couplings, (1,), after, 8)
    down = product_rows(couplings, (0,), after, 0)
    chord_products(up, down, odd_ref, even_ref)


def last_settle_kernel(
    part, chord_odd, chord_even, span_odd, span_even, masks, line_inverse, adjoint, after_ref, residual_ref
):
    residual, after = settle(part, (chord_odd, chord_even, span_odd, span_even), masks, line_inverse, adjoint)
    for a in range(6):
        after_ref[a] = after[a]
        residual_ref[a] = residual[a]


def cut_change(cut, chord_odd, masks, line_inverse):
    arrived = jnp.where(beside_mirror(), chord_odd[6, :, 0:128], cut[...])
    wake = masks[2] > 0
    lane = iotas((16, 128))[1]
    columns = []
    for b in range(6):
        slabs = [pltpu.roll(arrived, (128 - 4 * b - 2 * c) % 128, 1) for c in (1, 0)]
        columns.append(jnp.where(wake, -jnp.concatenate(slabs, axis=0), 0.0))
    change = [jnp.where(lane == 0, column, 0.0) for column in columns]
    delta = []
    for a in range(6):
        total = None
        for b in range(6):
            term = line_inverse[a, b, 0, :, 0:128].astype(F32) * columns[b]
            total = term if b == 0 else total + term
        delta.append(jnp.where(lane < 2, total, 0.0))
    return change, delta


def cut_kernel(
    cut, chord_odd, masks, line_inverse, couplings, main, odd, even, after_ref, cut_ref, chord_odd_ref, chord_even_ref
):
    _, delta = cut_change(cut, chord_odd, masks, line_inverse)
    near = [main[a, :, 0:128] + delta[a] for a in range(6)]
    for a in range(6):
        after_ref[a, :, 0:128] = near[a]
        after_ref[a, :, 128:256] = main[a, :, 128:256]
    row = cut_row(couplings, near)
    cut_ref[...] = row
    chord_odd_ref[6, :, 0:128] = row
    chord_odd_ref[0:6] = odd[...]
    chord_even_ref[...] = even[...]
    up = product_rows(couplings, (1,), delta, 8, 128)
    down = product_rows(couplings, (0,), delta, 0, 128)
    even_chord = lax.axis_index("chord") % 2 == 0
    inner_chord = inner("chord")
    for b in range(6):
        first = jnp.where(inner_chord, jnp.where(even_chord, down[b], up[b]), 0.0)
        chord_odd_ref[b, :, 0:128] = odd[b, :, 0:128] + first
        chord_even_ref[b, :, 0:128] = even[b, :, 0:128] + jnp.where(even_chord, up[b], down[b])


def last_cut_kernel(
    cut, chord_odd, masks, line_inverse, main, held, after_ref, residual_ref, after_scratch, residual_scratch, sems
):
    change, delta = cut_change(cut, chord_odd, masks, line_inverse)
    copies = []
    for i, (old, added, scratch, to) in enumerate(
        ((held, change, residual_scratch, residual_ref), (main, delta, after_scratch, after_ref))
    ):
        for a in range(6):
            scratch[a, :, 0:128] = old[a, :, 0:128] + added[a]
            scratch[a, :, 128:256] = old[a, :, 128:256]
        copies.append(pltpu.make_async_copy(scratch, to, sems.at[i]))
        copies[-1].start()
    for copy in copies:
        copy.wait()


def call(kernel, name, operands, shapes, flops, in_vmem=True):
    vmem = pl.BlockSpec(memory_space=pltpu.VMEM)
    space = pltpu.VMEM if in_vmem else pltpu.HBM
    held = [pltpu.with_memory_space_constraint(x, pltpu.VMEM) for x in operands]
    return pl.pallas_call(
        kernel,
        name=name,
        out_shape=[space(s, F32) for s in shapes],
        in_specs=[vmem] * len(held),
        out_specs=[pl.BlockSpec(memory_space=space)] * len(shapes),
        scratch_shapes=[] if in_vmem else [*(pltpu.VMEM(s, F32) for s in shapes), pltpu.SemaphoreType.DMA((2,))],
        compiler_params=pltpu.CompilerParams(vmem_limit_bytes=VMEM_LIMIT),
        cost_estimate=pl.CostEstimate(flops=flops, bytes_accessed=0, transcendentals=0),
    )(*held)


FIELD = (6, 16, 256)
SLAB = (6, 8, 256)
ROWS = (16, 256)
FIRST = [(8, 128), (7, 8, 256), SLAB]
SECOND = [ROWS, (24, 256)]


def load(couplings, adjoint):
    vmem = pl.BlockSpec(memory_space=pltpu.VMEM)
    operands = [
        pltpu.with_memory_space_constraint(x, pltpu.HBM) for x in (couplings, adjoint)
    ]
    held = [pltpu.VMEM(x.shape, x.dtype) for x in (adjoint, couplings)]
    return pl.pallas_call(
        load_kernel,
        name="load",
        out_shape=[*held, *(pltpu.VMEM(s, F32) for s in FIRST)],
        in_specs=[pl.BlockSpec(memory_space=pltpu.HBM)] * 2,
        out_specs=[vmem] * 5,
        scratch_shapes=[pltpu.SemaphoreType.DMA((5,))],
        compiler_params=pltpu.CompilerParams(vmem_limit_bytes=VMEM_LIMIT),
        cost_estimate=pl.CostEstimate(flops=1_000_000, bytes_accessed=0, transcendentals=0),
    )(*operands)


def pairs(chords, spans, axis, start):
    found = []
    for chord in range(chords):
        for span in range(spans):
            index, count = (chord, chords) if axis == "chord" else (span, spans)
            other = index + 1 if (index - start) % 2 == 0 else index - 1
            if 0 <= other < count:
                to = (other, span) if axis == "chord" else (chord, other)
            else:
                to = (chord, span ^ 1) if axis == "chord" else (chord ^ 1, span)
            found.append((chord * spans + span, to[0] * spans + to[1]))
    return found


def mirrors(chords, spans):
    found = []
    for chord in range(chords):
        for span in range(spans):
            if abs(2 * chord + 1 - chords) == 1:
                to = (chord, span ^ 1)
            else:
                to = (chords - 1 - chord, span)
            found.append((chord * spans + span, to[0] * spans + to[1]))
    return found


def exchange(sent):
    cut, chord_odd, chord_even, span_odd, span_even = sent
    chords, spans = lax.axis_size("chord"), lax.axis_size("span")
    cut = lax.ppermute(cut, ("chord", "span"), mirrors(chords, spans))
    chord_odd = lax.ppermute(chord_odd, ("chord", "span"), pairs(chords, spans, "chord", 1))
    chord_even = lax.ppermute(chord_even, ("chord", "span"), pairs(chords, spans, "chord", 0))
    span_odd = lax.ppermute(span_odd, ("chord", "span"), pairs(chords, spans, "span", 1))
    span_even = lax.ppermute(span_even, ("chord", "span"), pairs(chords, spans, "span", 0))
    return cut, chord_odd, chord_even, span_odd, span_even


def per_device(adjoint, source, diag_block, couplings, line_inverse, partner, codes):
    adjoint = adjoint.reshape(FIELD)
    source = source.reshape(FIELD)
    diag_block = diag_block.reshape(6, 6, 16, 256)
    couplings = couplings.reshape(6, 6, 6, 16, 256)
    line_inverse = line_inverse.reshape(6, 6, 2, 16, 256)
    adjoint, couplings, *far = load(couplings, adjoint)
    for sweep in range(SWEEPS):
        near = call(edges_kernel, "edges", (adjoint, couplings), SECOND, 1_000)
        got = exchange((*far, *near))
        held = (near[0], source, diag_block, couplings, adjoint)
        if sweep == 0:
            part, masks = call(
                first_inside_kernel, "inside_masks", (*held, partner.reshape(1, 2), codes), [FIELD, (3, 16, 128)], INSIDE
            )
        else:
            [part] = call(inside_kernel, "inside", held, [FIELD], INSIDE)
        cut, *beside = got
        arguments = (part, *beside, masks, line_inverse, adjoint)
        late = (cut, beside[0], masks, line_inverse)
        if sweep < SWEEPS - 1:
            main, odd, even = call(settle_kernel, "settle", (*arguments, couplings), [FIELD, SLAB, SLAB], SETTLE)
            adjoint, *far = call(cut_kernel, "cut", (*late, couplings, main, odd, even), [FIELD, *FIRST], 1_000)
        else:
            main, held = call(last_settle_kernel, "last_settle", arguments, [FIELD, FIELD], SETTLE)
            adjoint, residual = call(last_cut_kernel, "last", (*late, main, held), [FIELD, FIELD], 1_000, False)
    return adjoint.reshape(6, 2, 8, 256), residual.reshape(6, 2, 8, 256)


def solution(mesh):
    placed = (
        P(None, "chord", "span", None),
        P(None, "chord", "span", None),
        P(None, None, "chord", "span", None),
        P(None, None, None, "chord", "span", None),
        P(None, None, None, "chord", "span", None),
        P("chord"),
        P("chord", "span"),
    )
    return jax.shard_map(
        per_device,
        mesh=mesh,
        in_specs=placed,
        out_specs=(P(None, "chord", "span", None), P(None, "chord", "span", None)),
        check_vma=False,
    )
```

```python
import jax
import jax.numpy as jnp
from jax import lax
from jax.experimental import pallas as pl
from jax.experimental.pallas import tpu as pltpu
from jax.sharding import PartitionSpec as P

SWEEPS = 6
F32 = jnp.float32
VMEM_LIMIT = 24 * 2**20
SETTLE = 1_000
INSIDE = 400_000_000


def product(blocks, lead, field):
    out = [None] * 6
    for a in range(6):
        for b in range(6):
            term = blocks[(*lead, a, b)].astype(F32) * field[a]
            out[b] = term if a == 0 else out[b] + term
    return out


def product_rows(blocks, lead, field, low, lanes=256):
    out = [None] * 6
    for a in range(6):
        for b in range(6):
            block = blocks[(*lead, a, b, slice(None), slice(0, lanes))].astype(F32)
            term = block[low : low + 8] * field[a][low : low + 8]
            out[b] = term if a == 0 else out[b] + term
    return out


def product_lanes(blocks, lead, field):
    out = [None] * 6
    for a in range(6):
        for b in range(6):
            term = blocks[(*lead, a, b, slice(None), slice(0, 128))].astype(F32) * field[a][:, 0:128]
            out[b] = term if a == 0 else out[b] + term
    return out


def inner(axis):
    index = lax.axis_index(axis)
    return (index > 0) & (index < lax.axis_size(axis) - 1)


def beside_mirror():
    half = lax.axis_size("chord") // 2
    index = lax.axis_index("chord")
    return (index == half - 1) | (index == half)


def iotas(shape):
    return lax.broadcasted_iota(jnp.int32, shape, 0), lax.broadcasted_iota(jnp.int32, shape, 1)


def cut_row(couplings, field):
    normal = product_lanes(couplings, (4,), field)
    lane = iotas((8, 128))[1]
    row = jnp.zeros((8, 128), F32)
    for b in range(6):
        for c in range(2):
            column = normal[b][8 * c : 8 * c + 8, 0:1]
            row = jnp.where(lane // 2 == 2 * b + c, column, row)
    return row


def chord_products(up, down, odd_ref, even_ref):
    even_chord = lax.axis_index("chord") % 2 == 0
    inner_chord = inner("chord")
    for b in range(6):
        odd_ref[b] = jnp.where(inner_chord, jnp.where(even_chord, down[b], up[b]), 0.0)
        even_ref[b] = jnp.where(even_chord, up[b], down[b])


def first_out(couplings, field, out):
    cut_ref, chord_odd_ref, chord_even_ref = out
    row = cut_row(couplings, field)
    cut_ref[...] = row
    chord_odd_ref[6, :, 0:128] = row
    up = product_rows(couplings, (1,), field, 8)
    down = product_rows(couplings, (0,), field, 0)
    chord_products(up, down, chord_odd_ref, chord_even_ref)


def edges_kernel(adjoint, couplings, span_odd_ref, span_even_ref):
    even_span = lax.axis_index("span") % 2 == 0
    inner_span = inner("span")
    last = iotas((16, 256))[0] % 8 == 7
    made = [None] * 6
    for a in range(6):
        for b in range(6):
            block = jnp.where(last, couplings[3, a, b], couplings[2, a, b]).astype(F32)
            term = block * adjoint[a]
            made[b] = term if a == 0 else made[b] + term
    for b in range(6):
        for c in range(2):
            top, bottom = (made[b][8 * c : 8 * c + 1], made[b][8 * c + 7 : 8 * c + 8])
            at = 2 * b + c
            span_odd_ref[at : at + 1] = jnp.where(inner_span, jnp.where(even_span, top, bottom), 0.0)
            span_even_ref[at : at + 1] = jnp.where(even_span, bottom, top)


def load_kernel(couplings, adjoint, *out):
    *held, cut_ref, chord_odd_ref, chord_even_ref, sems = out
    held_adjoint, held_couplings = held
    moved = [(adjoint, held_adjoint, slice(None))]
    moved += [(couplings, held_couplings, pl.ds(low, high - low)) for low, high in ((0, 2), (4, 5), (2, 4), (5, 6))]
    copies = [pltpu.make_async_copy(a.at[i], b.at[i], sems.at[n]) for n, (a, b, i) in enumerate(moved)]
    for copy in copies:
        copy.start()
    for copy in copies[:3]:
        copy.wait()
    field = [held_adjoint[a] for a in range(6)]
    first_out(held_couplings, field, (cut_ref, chord_odd_ref, chord_even_ref))
    for copy in copies[3:]:
        copy.wait()


def inside_kernel(sent, source, diag_block, couplings, adjoint, out):
    field = [adjoint[a] for a in range(6)]
    row, lane = iotas((16, 256))
    row = row % 8
    span_plus = product(couplings, (3,), field)
    span_minus = product(couplings, (2,), field)
    for b in range(6):
        inside = jnp.where(row == 0, 0.0, pltpu.roll(span_plus[b], 1, 0))
        inside = inside + jnp.where(row == 7, 0.0, pltpu.roll(span_minus[b], 15, 0))
        out[b] = source[b] - inside
    own = product(diag_block, (), field)
    up = product_rows(couplings, (1,), field, 0)
    down = product_rows(couplings, (0,), field, 8)
    plus = product(couplings, (5,), field)
    minus = product(couplings, (4,), field)
    for b in range(6):
        inside = own[b] + jnp.where(lane == 0, 0.0, pltpu.roll(plus[b], 1, 1))
        inside = inside + jnp.where(lane == 255, 0.0, pltpu.roll(minus[b], 255, 1))
        inside = inside + jnp.concatenate([down[b], up[b]], axis=0)
        out[b] = out[b] - inside


def first_inside_kernel(sent, source, diag_block, couplings, adjoint, partner, codes, out, masks_ref):
    inside_kernel(sent, source, diag_block, couplings, adjoint, out)
    here, there = iotas((8, 8))
    for c in range(2):
        rows = jnp.broadcast_to(codes[c : c + 1, :], (8, 8))
        code = jnp.sum(jnp.where(here == there, rows, 0), axis=1, keepdims=True)
        wall = jnp.broadcast_to(partner[:, c : c + 1], (8, 1)) < 0
        factors = (
            jnp.where(wall & (code == 0), 0.0, 1.0),
            jnp.where(wall, 0.0, 1.0),
            jnp.where(wall, 0.0, 1.0),
        )
        for i, factor in enumerate(factors):
            masks_ref[i, 8 * c : 8 * c + 8, :] = jnp.broadcast_to(factor.astype(F32), (8, 128))


def sweep_residual(part, got, masks, even_chord, even_span):
    chord_odd, chord_even, span_odd, span_even = got
    row, lane = iotas((16, 256))
    row = row % 8
    top = jnp.where(even_span, span_odd[...], span_even[0:16])
    bottom = jnp.where(even_span, span_even[0:16], span_odd[...])
    odd_lane = lane % 2 == 1
    residual, even_part, odd_part = [], [], []
    for b in range(6):
        ev, od = chord_even[b], chord_odd[b]
        outside = jnp.concatenate([jnp.where(even_chord, od, ev), jnp.where(even_chord, ev, od)], axis=0)
        tops = jnp.concatenate(
            [jnp.broadcast_to(top[2 * b + c : 2 * b + c + 1], (8, 256)) for c in range(2)], axis=0
        )
        bottoms = jnp.concatenate(
            [jnp.broadcast_to(bottom[2 * b + c : 2 * b + c + 1], (8, 256)) for c in range(2)], axis=0
        )
        outside = outside + jnp.where(row == 0, tops, jnp.where(row == 7, bottoms, 0.0))
        value = part[b] - outside
        if 1 <= b <= 3:
            value = value * jnp.where(lane == 0, masks[0][:, 0:1], 1.0)
        if b == 5:
            value = value * jnp.where(lane == 0, masks[1][:, 0:1], 1.0)
        residual.append(value)
        even_part.append(jnp.where(odd_lane, pltpu.roll(value, 1, 1), value))
        odd_part.append(jnp.where(odd_lane, value, pltpu.roll(value, 255, 1)))
    return residual, (even_part, odd_part)


def line_update(line_inverse, adjoint, parts, a):
    total = adjoint[a]
    for b in range(6):
        for q in range(2):
            total = total + line_inverse[a, b, q].astype(F32) * parts[q][b]
    return total


def settle(part, got, masks, line_inverse, adjoint):
    even_chord = lax.axis_index("chord") % 2 == 0
    even_span = lax.axis_index("span") % 2 == 0
    residual, parts = sweep_residual(part, got, masks, even_chord, even_span)
    return residual, [line_update(line_inverse, adjoint, parts, a) for a in range(6)]


def settle_kernel(
    part, chord_odd, chord_even, span_odd, span_even, masks, line_inverse, adjoint, couplings, after_ref, odd_ref, even_ref
):
    _, after = settle(part, (chord_odd, chord_even, span_odd, span_even), masks, line_inverse, adjoint)
    for a in range(6):
        after_ref[a] = after[a]
    up = product_rows(couplings, (1,), after, 8)
    down = product_rows(couplings, (0,), after, 0)
    chord_products(up, down, odd_ref, even_ref)


def last_settle_kernel(
    part, chord_odd, chord_even, span_odd, span_even, masks, line_inverse, adjoint, after_ref, residual_ref
):
    residual, after = settle(part, (chord_odd, chord_even, span_odd, span_even), masks, line_inverse, adjoint)
    for a in range(6):
        after_ref[a] = after[a]
        residual_ref[a] = residual[a]


def cut_change(cut, chord_odd, masks, line_inverse):
    arrived = jnp.where(beside_mirror(), chord_odd[6, :, 0:128], cut[...])
    wake = masks[2] > 0
    lane = iotas((16, 128))[1]
    columns = []
    for b in range(6):
        slabs = [pltpu.roll(arrived, (128 - 4 * b - 2 * c) % 128, 1) for c in (1, 0)]
        columns.append(jnp.where(wake, -jnp.concatenate(slabs, axis=0), 0.0))
    change = [jnp.where(lane == 0, column, 0.0) for column in columns]
    delta = []
    for a in range(6):
        total = None
        for b in range(6):
            term = line_inverse[a, b, 0, :, 0:128].astype(F32) * columns[b]
            total = term if b == 0 else total + term
        delta.append(jnp.where(lane < 2, total, 0.0))
    return change, delta


def cut_kernel(
    cut, chord_odd, masks, line_inverse, couplings, main, odd, even, after_ref, cut_ref, chord_odd_ref, chord_even_ref
):
    _, delta = cut_change(cut, chord_odd, masks, line_inverse)
    near = [main[a, :, 0:128] + delta[a] for a in range(6)]
    for a in range(6):
        after_ref[a, :, 0:128] = near[a]
        after_ref[a, :, 128:256] = main[a, :, 128:256]
    row = cut_row(couplings, near)
    cut_ref[...] = row
    chord_odd_ref[6, :, 0:128] = row
    chord_odd_ref[0:6] = odd[...]
    chord_even_ref[0:6] = even[...]
    up = product_rows(couplings, (1,), delta, 8, 128)
    down = product_rows(couplings, (0,), delta, 0, 128)
    even_chord = lax.axis_index("chord") % 2 == 0
    inner_chord = inner("chord")
    for b in range(6):
        first = jnp.where(inner_chord, jnp.where(even_chord, down[b], up[b]), 0.0)
        chord_odd_ref[b, :, 0:128] = odd[b, :, 0:128] + first
        chord_even_ref[b, :, 0:128] = even[b, :, 0:128] + jnp.where(even_chord, up[b], down[b])


def last_cut_kernel(
    cut, chord_odd, masks, line_inverse, main, held, after_ref, residual_ref, after_scratch, residual_scratch, sems
):
    change, delta = cut_change(cut, chord_odd, masks, line_inverse)
    copies = []
    for i, (old, added, scratch, to) in enumerate(
        ((held, change, residual_scratch, residual_ref), (main, delta, after_scratch, after_ref))
    ):
        for a in range(6):
            scratch[a, :, 0:128] = old[a, :, 0:128] + added[a]
            scratch[a, :, 128:256] = old[a, :, 128:256]
        copies.append(pltpu.make_async_copy(scratch, to, sems.at[i]))
        copies[-1].start()
    for copy in copies:
        copy.wait()


def call(kernel, name, operands, shapes, flops, in_vmem=True):
    vmem = pl.BlockSpec(memory_space=pltpu.VMEM)
    space = pltpu.VMEM if in_vmem else pltpu.HBM
    held = [pltpu.with_memory_space_constraint(x, pltpu.VMEM) for x in operands]
    return pl.pallas_call(
        kernel,
        name=name,
        out_shape=[space(s, F32) for s in shapes],
        in_specs=[vmem] * len(held),
        out_specs=[pl.BlockSpec(memory_space=space)] * len(shapes),
        scratch_shapes=[] if in_vmem else [*(pltpu.VMEM(s, F32) for s in shapes), pltpu.SemaphoreType.DMA((2,))],
        compiler_params=pltpu.CompilerParams(vmem_limit_bytes=VMEM_LIMIT),
        cost_estimate=pl.CostEstimate(flops=flops, bytes_accessed=0, transcendentals=0),
    )(*held)


FIELD = (6, 16, 256)
SLAB = (6, 8, 256)
ROWS = (16, 256)
FIRST = [(8, 128), (7, 8, 256), (8, 8, 256)]
SECOND = [ROWS, (24, 256)]


def load(couplings, adjoint):
    vmem = pl.BlockSpec(memory_space=pltpu.VMEM)
    operands = [
        pltpu.with_memory_space_constraint(x, pltpu.HBM) for x in (couplings, adjoint)
    ]
    held = [pltpu.VMEM(x.shape, x.dtype) for x in (adjoint, couplings)]
    return pl.pallas_call(
        load_kernel,
        name="load",
        out_shape=[*held, *(pltpu.VMEM(s, F32) for s in FIRST)],
        in_specs=[pl.BlockSpec(memory_space=pltpu.HBM)] * 2,
        out_specs=[vmem] * 5,
        scratch_shapes=[pltpu.SemaphoreType.DMA((5,))],
        compiler_params=pltpu.CompilerParams(vmem_limit_bytes=VMEM_LIMIT),
        cost_estimate=pl.CostEstimate(flops=1_000_000, bytes_accessed=0, transcendentals=0),
    )(*operands)


def pairs(chords, spans, axis, start):
    found = []
    for chord in range(chords):
        for span in range(spans):
            index, count = (chord, chords) if axis == "chord" else (span, spans)
            other = index + 1 if (index - start) % 2 == 0 else index - 1
            if 0 <= other < count:
                to = (other, span) if axis == "chord" else (chord, other)
            else:
                to = (chord, span ^ 1) if axis == "chord" else (chord ^ 1, span)
            found.append((chord * spans + span, to[0] * spans + to[1]))
    return found


def mirrors(chords, spans):
    found = []
    for chord in range(chords):
        for span in range(spans):
            if abs(2 * chord + 1 - chords) == 1:
                to = (chord, span ^ 1)
            else:
                to = (chords - 1 - chord, span)
            found.append((chord * spans + span, to[0] * spans + to[1]))
    return found


def exchange(sent):
    cut, chord_odd, chord_even, span_odd, span_even = sent
    chords, spans = lax.axis_size("chord"), lax.axis_size("span")
    cut = lax.ppermute(cut, ("chord", "span"), mirrors(chords, spans))
    chord_odd = lax.ppermute(chord_odd, ("chord", "span"), pairs(chords, spans, "chord", 1))
    chord_even = lax.ppermute(chord_even, ("chord", "span"), pairs(chords, spans, "chord", 0))
    span_odd = lax.ppermute(span_odd, ("chord", "span"), pairs(chords, spans, "span", 1))
    span_even = lax.ppermute(span_even, ("chord", "span"), pairs(chords, spans, "span", 0))
    return cut, chord_odd, chord_even, span_odd, span_even


def per_device(adjoint, source, diag_block, couplings, line_inverse, partner, codes):
    adjoint = adjoint.reshape(FIELD)
    source = source.reshape(FIELD)
    diag_block = diag_block.reshape(6, 6, 16, 256)
    couplings = couplings.reshape(6, 6, 6, 16, 256)
    line_inverse = line_inverse.reshape(6, 6, 2, 16, 256)
    adjoint, couplings, *far = load(couplings, adjoint)
    for sweep in range(SWEEPS):
        near = call(edges_kernel, "edges", (adjoint, couplings), SECOND, 1_000)
        got = exchange((*far, *near))
        held = (near[0], source, diag_block, couplings, adjoint)
        if sweep == 0:
            part, masks = call(
                first_inside_kernel, "inside_masks", (*held, partner.reshape(1, 2), codes), [FIELD, (3, 16, 128)], INSIDE
            )
        else:
            [part] = call(inside_kernel, "inside", held, [FIELD], INSIDE)
        cut, *beside = got
        arguments = (part, *beside, masks, line_inverse, adjoint)
        late = (cut, beside[0], masks, line_inverse)
        if sweep < SWEEPS - 1:
            main, odd, even = call(settle_kernel, "settle", (*arguments, couplings), [FIELD, SLAB, SLAB], SETTLE)
            adjoint, *far = call(cut_kernel, "cut", (*late, couplings, main, odd, even), [FIELD, *FIRST], 1_000)
        else:
            main, held = call(last_settle_kernel, "last_settle", arguments, [FIELD, FIELD], SETTLE)
            adjoint, residual = call(last_cut_kernel, "last", (*late, main, held), [FIELD, FIELD], 1_000, False)
    return adjoint.reshape(6, 2, 8, 256), residual.reshape(6, 2, 8, 256)


def solution(mesh):
    placed = (
        P(None, "chord", "span", None),
        P(None, "chord", "span", None),
        P(None, None, "chord", "span", None),
        P(None, None, None, "chord", "span", None),
        P(None, None, None, "chord", "span", None),
        P("chord"),
        P("chord", "span"),
    )
    return jax.shard_map(
        per_device,
        mesh=mesh,
        in_specs=placed,
        out_specs=(P(None, "chord", "span", None), P(None, "chord", "span", None)),
        check_vma=False,
    )
```
